32 devices in a mesh: task: 4 (over y, core), rows: 8 (over z, x).
Axes of the slice: x: 2, y: 2, z: 4, core: 2. Of those that a mesh axis runs over, the one named last changes fastest.
Arguments:
- probes: bfloat16 [4, 384, 8192], P('task', None, 'rows'), may hold values from -48 to 48
- task_weights: bfloat16 [4, 8192, 128], P('task', 'rows'), may hold values from -6 to 6
Outputs:
- merged: float32 [8192, 128], P(('rows', 'task'))
- residual: float32 [8192, 128], P(('rows', 'task'))
The draws below stay inside these ranges and needn't reach their ends.
All inputs are finite; a program needn't handle non-finite values.
Results may differ from the reference program's by a relative error of at most 0.0003.
Values may be sent and summed in bfloat16 or wider, within the bound.
A program may use at most 128 MiB of HBM per device.

```python
import math
import jax
import jax.numpy as jnp
from jax import lax

D = 8192
PROBE = 384
COLS = 128
ITERS = 2
TASKS = 4


def draw_probes(key, part):
    k_base, k_col, k_row = jax.random.split(key, 3)
    ramp = jnp.arange(D, dtype=jnp.float32) / max(D - 1, 1)
    colscale = (1.0 + 2.0 * ramp) * jnp.exp(jax.random.uniform(k_col, (D,), jnp.float32, 0.0, math.log(3.0))) / 3.0
    rowscale = jnp.exp(jax.random.uniform(k_row, (TASKS, PROBE, 1), jnp.float32, 0.0, math.log(4.0))) / 2.0
    base = jnp.clip(jax.random.normal(k_base, (TASKS, PROBE, D), jnp.float32), -5.0, 5.0)
    return (base * rowscale * colscale[None, None, :]).astype(jnp.bfloat16)


def steps_of(own_key, dims, cuts, least, top_value):
    level = 1.0
    for dim, parts in cuts:
        draws = jax.random.uniform(jax.random.fold_in(jax.random.fold_in(own_key, 6), dim), (parts,), jnp.float32, least / len(cuts), top_value / len(cuts))
        level = level * jnp.repeat(jnp.exp(draws), dims[dim] // parts).reshape((-1,) + (1,) * (len(dims) - 1 - dim))
    return level


def bell_draw(stream_key, dims, scale, bound, cuts=(), kind=jnp.bfloat16):
    result = jax.random.normal(stream_key, dims, jnp.float32) * scale
    if len(cuts) > 0:
        result = steps_of(stream_key, dims, cuts, -0.22, 0.18) * result
    return jnp.clip(result, min=-bound, max=bound).astype(kind)


def setup_inputs(seed: int = 0) -> dict:
    streams_of = jax.random.split(jax.random.key(seed), 3)
    probes = draw_probes(jax.random.fold_in(streams_of[2], 71), 0)
    task_weights = bell_draw(streams_of[1], (TASKS, D, COLS), 1.0, 6.0, ((0, 4), (1, 8)))
    return dict(probes=probes, task_weights=task_weights)


ALPHA = 0.9
EPS = 1e-6


def reference(probes, task_weights):
    scale = 1.0 / (PROBE * TASKS)

    def accumulate(carry, item):
        acc_sys, acc_tgt, acc_diag = carry
        x, w = item
        g = jnp.dot(x.T, x, preferred_element_type=jnp.float32)
        d = jnp.diagonal(g)
        y = jnp.dot(x, w, preferred_element_type=jnp.float32)
        b = ALPHA * jnp.einsum("pd,pc->dc", x.astype(jnp.float32), y, precision=lax.Precision.HIGHEST)
        b = b + (1.0 - ALPHA) * d[:, None] * w.astype(jnp.float32)
        return (acc_sys + (ALPHA * scale) * g, acc_tgt + scale * b, acc_diag + ((1.0 - ALPHA) * scale) * d), None

    init = (jnp.zeros((D, D), jnp.float32), jnp.zeros((D, COLS), jnp.float32), jnp.zeros((D,), jnp.float32))
    (system, targets, diag_sum), _ = lax.scan(accumulate, init, (probes, task_weights))
    idx = jnp.arange(D, dtype=jnp.int32)
    system = system.at[idx, idx].add(diag_sum)

    merged = jnp.zeros((D, COLS), jnp.float32)
    residual = targets
    direction = targets
    norm_now = jnp.sum(residual * residual, axis=0)
    for step in range(ITERS):
        image = jnp.dot(system, direction, precision=lax.Precision.HIGHEST)
        alpha = norm_now / jnp.sum(direction * image, axis=0)
        merged = merged + alpha * direction
        residual = residual - alpha * image
        norm_next = jnp.sum(residual * residual, axis=0)
        direction = residual + (norm_next / (norm_now + EPS)) * direction
        norm_now = norm_next
    return merged, residual
```

```python
import functools

import jax
import jax.numpy as jnp
from jax import lax
from jax.experimental import pallas as pl
from jax.experimental.pallas import tpu as pltpu
from jax.sharding import PartitionSpec as P

ALPHA = 0.9
EPS = 1e-06
LANES = 128
SUB = 8
CHUNKS = 4
F32 = jnp.float32
BF16 = jnp.bfloat16
MESH = pl.DeviceIdType.MESH


def two_terms(value):
    high = value.astype(BF16).astype(F32)
    return jnp.concatenate([high, value - high], axis=0).astype(BF16)


def fold(product):
    half = product.shape[0] // 2
    return product[:half] + product[half:]


def times_probes(value, xs):
    return fold(jnp.dot(two_terms(value), xs[...], preferred_element_type=F32))


def times_features(value, xs):
    return fold(
        lax.dot_general(
            two_terms(value), xs[...], (((1,), (1,)), ((), ())), preferred_element_type=F32
        )
    )


def remote(src, dst, send, recv, device):
    return pltpu.make_async_remote_copy(
        src_ref=src, dst_ref=dst, send_sem=send, recv_sem=recv, device_id=device, device_id_type=MESH
    )


def kernel(
    tasks, rows,
    x_hbm, w_hbm, merged_ref, residual_ref,
    xs, w_own, wt_send, wt_all, y_send, y_recv, y_red, y_all,
    z_send, z_recv, z_red, z_full, z_flat, fin_send, fin_recv,
    local_sem, cross_send, cross_recv, core_send, core_recv, w_send_sem, w_recv_sem,
    yr_send, yr_recv, ya_send, ya_recv, zr_send, zr_recv, za_send, za_recv, f_send, f_recv,
):
    t, r = lax.axis_index("task"), lax.axis_index("rows")
    probe, width = x_hbm.shape[1:]
    cols = w_hbm.shape[2]
    group = cols // tasks
    piece = cols // rows
    per = group // piece
    parts = rows // (group // SUB)
    span = tasks * probe // parts
    share = width // tasks
    pairs = tasks // 2
    chunk = probe // CHUNKS
    c1 = ALPHA / (probe * tasks)
    c2 = (1.0 - ALPHA) / (probe * tasks)
    total = tasks * rows

    barrier = pltpu.get_barrier_semaphore()
    me = t * rows + r

    @pl.loop(1, total)
    def _(i):
        other = lax.rem(me + i, total)
        pl.semaphore_signal(
            barrier, inc=1, device_id=(other // rows, lax.rem(other, rows)), device_id_type=MESH
        )

    load_x = pltpu.make_async_copy(
        x_hbm.at[0], xs.at[pl.ds(pl.multiple_of(t * probe, probe), probe)], local_sem.at[0]
    )
    load_x.start()
    load_w = pltpu.make_async_copy(w_hbm.at[0], w_own, local_sem.at[1])
    load_w.start()
    pl.semaphore_wait(barrier, total - 1)

    pair, core = t // 2, lax.rem(t, 2)
    mate = (pair * 2 + 1 - core, r)

    def rows_of(task, c):
        return pl.ds(pl.multiple_of(task * probe + c * chunk, chunk), chunk)

    def cross(j, c):
        to = (lax.rem(pair + j, pairs) * 2 + core, r)
        return remote(
            x_hbm.at[0, pl.ds(c * chunk, chunk)], xs.at[rows_of(t, c)],
            cross_send.at[j, c], cross_recv.at[j, c], to,
        )

    def crossed(j, c):
        return xs.at[rows_of(lax.rem(pair - j + pairs, pairs) * 2 + core, c)]

    def arrived(j, c):
        place = crossed(j, c)
        return remote(place, place, cross_send.at[j, c], cross_recv.at[j, c], mate)

    def own_to_mate(c):
        return remote(
            x_hbm.at[0, pl.ds(c * chunk, chunk)], xs.at[rows_of(t, c)],
            core_send.at[0, c], core_recv.at[0, c], mate,
        )

    def relay(j, c):
        place = crossed(j, c)
        return remote(place, place, core_send.at[j, c], core_recv.at[j, c], mate)

    def from_mate(j, c):
        source = lax.rem(pair - j + pairs, pairs) * 2 + 1 - core
        place = xs.at[rows_of(source, c)]
        return remote(place, place, core_send.at[j, c], core_recv.at[j, c], mate)

    for c in range(CHUNKS):
        for j in range(1, pairs):
            cross(j, c).start()
    for c in range(CHUNKS):
        own_to_mate(c).start()

    load_w.wait()
    load_x.wait()
    own = xs[pl.ds(pl.multiple_of(t * probe, probe), probe), :]
    outputs = jnp.dot(own, w_own[...], preferred_element_type=F32)
    y_send[...] = outputs.T.reshape(y_send.shape)

    def y_scatter(k):
        to = lax.rem(r + k, rows)
        return remote(y_send.at[to], y_recv.at[k], yr_send.at[k], yr_recv.at[k], (t, to))

    for k in range(1, rows):
        y_scatter(k).start()

    wt_send[...] = w_own[...].astype(F32).T.reshape(wt_send.shape).astype(wt_send.dtype)

    def w_scatter(j):
        to = lax.rem(t + j, tasks)
        return remote(wt_send.at[to], wt_all.at[t], w_send_sem.at[j], w_recv_sem.at[j], (to, r))

    for j in range(1, tasks):
        w_scatter(j).start()
    wt_all[t] = wt_send[t]

    total_y = y_send[r]
    for k in range(1, rows):
        y_scatter(k).wait_recv()
        total_y = total_y + y_recv[k]
    y_red[...] = total_y
    owner = r // per
    place_y = y_all.at[
        pl.ds(pl.multiple_of(lax.rem(r, per) * piece, piece), piece),
        pl.ds(pl.multiple_of(t * probe, LANES), probe),
    ]

    def y_gather(k):
        return remote(
            y_red, place_y, ya_send.at[k], ya_recv.at[t * per + lax.rem(r, per)],
            (owner, lax.rem(r + k, rows)),
        )

    for k in range(1, rows):
        y_gather(k).start()

    @pl.when(owner != t)
    def _():
        y_gather(0).start()

    @pl.when(owner == t)
    def _():
        y_all[
            pl.ds(pl.multiple_of(lax.rem(r, per) * piece, piece), piece),
            pl.ds(pl.multiple_of(t * probe, LANES), probe),
        ] = total_y

    for c in range(CHUNKS):
        for j in range(1, pairs):
            arrived(j, c).wait_recv()
            relay(j, c).start()
    for c in range(CHUNKS):
        for j in range(pairs):
            from_mate(j, c).wait_recv()
    for j in range(1, tasks):
        source = lax.rem(t - j + tasks, tasks)
        remote(
            wt_send.at[0], wt_all.at[source], w_send_sem.at[j], w_recv_sem.at[j], (t, r)
        ).wait_recv()

    diag = jnp.zeros((1, width), F32)
    term = jnp.zeros((group, width), F32)
    for task in range(tasks):

        def squares(i, acc):
            block = xs[pl.ds(pl.multiple_of(task * probe + i * 16, 16), 16), :].astype(F32)
            return acc + block * block

        own_diag = jnp.sum(
            lax.fori_loop(0, probe // 16, squares, jnp.zeros((16, width), F32)), axis=0, keepdims=True
        )
        diag = diag + own_diag
        term = term + own_diag * wt_all[task].astype(F32)
    diag = c2 * diag

    for task in range(tasks):
        for k in range(per):

            @pl.when(jnp.logical_or(task != t, t * per + k != r))
            def _():
                place = y_all.at[pl.ds(k * piece, piece), pl.ds(task * probe, probe)]
                remote(
                    y_red, place, ya_send.at[0], ya_recv.at[task * per + k], (t, r)
                ).wait_recv()

    targets = c1 * times_probes(y_all[...], xs) + c2 * term

    lane = lax.broadcasted_iota(jnp.int32, (group, LANES), 1)

    def reduce_rows(n, product, sums):
        extra = jnp.zeros((group, LANES), F32)
        for i, value in enumerate(sums):
            extra = jnp.where(lane == i, value, extra)
        for q in range(rows):
            top, left = SUB * (q // parts), span * (q % parts)
            z_send[n, q, :, :span] = product[top : top + SUB, left : left + span]
            z_send[n, q, :, span:] = extra[top : top + SUB]

        def scatter(k):
            to = lax.rem(r + k, rows)
            return remote(
                z_send.at[n, to], z_recv.at[n, k], zr_send.at[n, k], zr_recv.at[n, k], (t, to)
            )

        for k in range(1, rows):
            scatter(k).start()
        acc = z_send[n, r]
        for k in range(1, rows):
            scatter(k).wait_recv()
            acc = acc + z_recv[n, k]
        z_red[n] = acc

        def gather(k):
            return remote(
                z_red.at[n], z_full.at[n, r], za_send.at[n, k], za_recv.at[n, k],
                (t, lax.rem(r + k, rows)),
            )

        for k in range(1, rows):
            gather(k).start()
        z_full[n, r] = acc
        for k in range(1, rows):
            source = lax.rem(r - k + rows, rows)
            remote(
                z_red.at[n], z_full.at[n, source], za_send.at[n, k], za_recv.at[n, k], (t, r)
            ).wait_recv()
        for q in range(rows):
            top, left = SUB * (q // parts), span * (q % parts)
            z_flat[n, top : top + SUB, left : left + span] = z_full[n, q, :, :span]
        found = jnp.concatenate(
            [z_full[n, q, :, span:] for q in range(0, rows, parts)], axis=0
        )
        for k in range(1, rows):
            scatter(k).wait_send()
            gather(k).wait_send()
        return z_flat[n], [found[:, i : i + 1] for i in range(len(sums))]

    def column_sum(value):
        return jnp.sum(value, axis=1, keepdims=True)

    product, (norm_0, weighted_00) = reduce_rows(
        0,
        times_features(targets, xs),
        [column_sum(targets * targets), column_sum(diag * targets * targets)],
    )
    step_1 = norm_0 / (c1 * column_sum(product * product) + weighted_00)
    residual = targets - step_1 * (c1 * times_probes(product, xs) + diag * targets)

    weighted = diag * residual
    product_r, (norm_1, weighted_11, weighted_01) = reduce_rows(
        1,
        times_features(residual, xs),
        [column_sum(residual * residual), column_sum(weighted * residual), column_sum(weighted * targets)],
    )
    beta = norm_1 / (norm_0 + EPS)
    product = product_r + beta * product
    direction = residual + beta * targets
    curve = c1 * column_sum(product * product) + (
        weighted_11 + beta * (2.0 * weighted_01 + beta * weighted_00)
    )
    step_2 = norm_1 / curve

    def finish(n, value):
        for q in range(tasks):
            fin_send[n, q, :, :share] = value[:, q * share : (q + 1) * share]
        for j in range(1, tasks):
            to = lax.rem(t + j, tasks)
            remote(
                fin_send.at[n, to], fin_recv.at[n, t], f_send.at[n, j], f_recv.at[n, j], (to, r)
            ).start()
        fin_recv[n, t] = fin_send[n, t]

    def collect(n, out_ref):
        for j in range(1, tasks):
            source = lax.rem(t - j + tasks, tasks)
            remote(
                fin_send.at[n, source], fin_recv.at[n, source], f_send.at[n, j], f_recv.at[n, j], (t, r)
            ).wait()
        whole = fin_recv[n].reshape(cols, fin_recv.shape[3]).T
        out_ref[...] = whole[:share]

    finish(0, step_1 * targets + step_2 * direction)
    finish(1, residual - step_2 * (c1 * times_probes(product, xs) + diag * direction))
    for c in range(CHUNKS):
        own_to_mate(c).wait_send()
        for j in range(1, pairs):
            cross(j, c).wait_send()
            relay(j, c).wait_send()
    for k in range(1, rows):
        y_scatter(k).wait_send()
        y_gather(k).wait_send()

    @pl.when(owner != t)
    def _():
        y_gather(0).wait_send()

    for j in range(1, tasks):
        w_scatter(j).wait_send()
    collect(0, merged_ref)
    collect(1, residual_ref)


def on_device(tasks, rows, probes, task_weights):
    probe, width = probes.shape[1:]
    cols = task_weights.shape[2]
    group = cols // tasks
    piece = cols // rows
    per = group // piece
    parts = rows // (group // SUB)
    span = tasks * probe // parts
    share = width // tasks
    pairs = tasks // 2
    padded = max(share, LANES)
    w_type = BF16 if group % 16 == 0 else F32
    vmem, dma = pltpu.VMEM, pltpu.SemaphoreType.DMA
    merged, residual = pl.pallas_call(
        functools.partial(kernel, tasks, rows),
        out_shape=[jax.ShapeDtypeStruct((share, cols), F32)] * 2,
        in_specs=[pl.BlockSpec(memory_space=pl.ANY)] * 2,
        out_specs=[pl.BlockSpec(memory_space=pltpu.VMEM)] * 2,
        scratch_shapes=[
            vmem((tasks * probe, width), BF16),
            vmem((width, cols), BF16),
            vmem((tasks, group, width), w_type),
            vmem((tasks, group, width), w_type),
            vmem((rows, piece, probe), F32),
            vmem((rows, piece, probe), F32),
            vmem((piece, probe), F32),
            vmem((group, tasks * probe), F32),
            vmem((2, rows, SUB, span + LANES), F32),
            vmem((2, rows, SUB, span + LANES), F32),
            vmem((2, SUB, span + LANES), F32),
            vmem((2, rows, SUB, span + LANES), F32),
            vmem((2, group, tasks * probe), F32),
            vmem((2, tasks, group, padded), F32),
            vmem((2, tasks, group, padded), F32),
            dma((2,)),
            dma((pairs, CHUNKS)),
            dma((pairs, CHUNKS)),
            dma((pairs, CHUNKS)),
            dma((pairs, CHUNKS)),
            dma((tasks,)),
            dma((tasks,)),
            dma((rows,)),
            dma((rows,)),
            dma((rows,)),
            dma((tasks * per,)),
            dma((2, rows)),
            dma((2, rows)),
            dma((2, rows)),
            dma((2, rows)),
            dma((2, tasks)),
            dma((2, tasks)),
        ],
        compiler_params=pltpu.CompilerParams(
            collective_id=0, has_side_effects=True, vmem_limit_bytes=48 * 2**20
        ),
    )(probes, task_weights)
    return merged, residual


def solution(mesh):
    in_specs = (P("task", None, "rows"), P("task", "rows", None))
    out_specs = (P(("rows", "task"), None), P(("rows", "task"), None))
    body = functools.partial(on_device, mesh.shape["task"], mesh.shape["rows"])
    return jax.shard_map(body, mesh=mesh, in_specs=in_specs, out_specs=out_specs, check_vma=False)
```

```python
import functools

import jax
import jax.numpy as jnp
from jax import lax
from jax.experimental import pallas as pl
from jax.experimental.pallas import tpu as pltpu
from jax.sharding import PartitionSpec as P

ALPHA = 0.9
EPS = 1e-06
LANES = 128
SUB = 8
CHUNKS = 6
F32 = jnp.float32
BF16 = jnp.bfloat16
MESH = pl.DeviceIdType.MESH


def two_terms(value):
    high = value.astype(BF16).astype(F32)
    return jnp.concatenate([high, value - high], axis=0).astype(BF16)


def fold(product):
    half = product.shape[0] // 2
    return product[:half] + product[half:]


def times_probes(value, xs):
    return fold(jnp.dot(two_terms(value), xs[...], preferred_element_type=F32))


def remote(src, dst, send, recv, device):
    return pltpu.make_async_remote_copy(
        src_ref=src, dst_ref=dst, send_sem=send, recv_sem=recv, device_id=device, device_id_type=MESH
    )


def kernel(
    tasks, rows,
    x_hbm, w_hbm, merged_ref, residual_ref,
    xs, w_own, wt_send, wt_all, y_send, y_recv, y_red, y_all,
    squares, z_send, z_recv, z_red, z_flat, fin_send, fin_recv,
    local_sem, cross_send, cross_recv, core_send, core_recv, w_send_sem, w_recv_sem,
    yr_send, yr_recv, ya_send, ya_recv, zr_send, zr_recv, za_send, za_recv, f_send, f_recv,
):
    t, r = lax.axis_index("task"), lax.axis_index("rows")
    probe, width = x_hbm.shape[1:]
    cols = w_hbm.shape[2]
    group = cols // tasks
    piece = cols // rows
    per = group // piece
    parts = rows // (group // SUB)
    span = tasks * probe // parts
    share = width // tasks
    pairs = tasks // 2
    chunk = probe // CHUNKS
    c1 = ALPHA / (probe * tasks)
    c2 = (1.0 - ALPHA) / (probe * tasks)

    barrier = pltpu.get_barrier_semaphore()

    @pl.loop(1, tasks)
    def _(i):
        pl.semaphore_signal(
            barrier, inc=1, device_id=(lax.rem(t + i, tasks), r), device_id_type=MESH
        )

    @pl.loop(1, rows)
    def _(i):
        pl.semaphore_signal(
            barrier, inc=1, device_id=(t, lax.rem(r + i, rows)), device_id_type=MESH
        )

    load_x = pltpu.make_async_copy(
        x_hbm.at[0], xs.at[pl.ds(pl.multiple_of(t * probe, probe), probe)], local_sem.at[0]
    )
    load_x.start()
    load_w = pltpu.make_async_copy(w_hbm.at[0], w_own, local_sem.at[1])
    load_w.start()

    def row_squares(first, count):
        def add(i, acc):
            block = xs[pl.ds(pl.multiple_of(first + i * 16, 16), 16), :].astype(F32)
            return acc + block * block

        return lax.fori_loop(0, count // 16, add, jnp.zeros((16, width), F32))

    load_w.wait()
    wt_send[...] = w_own[...].astype(F32).T.reshape(wt_send.shape).astype(wt_send.dtype)
    wt_all[t] = wt_send[t]
    load_x.wait()
    own = xs[pl.ds(pl.multiple_of(t * probe, probe), probe), :]
    outputs = jnp.dot(own, w_own[...], preferred_element_type=F32)
    y_send[...] = outputs.T.reshape(y_send.shape)
    squares[t] = row_squares(t * probe, probe)
    pl.semaphore_wait(barrier, tasks + rows - 2)

    pair, core = t // 2, lax.rem(t, 2)
    mate = (pair * 2 + 1 - core, r)

    def rows_of(task, c):
        return pl.ds(pl.multiple_of(task * probe + c * chunk, chunk), chunk)

    def cross(j, c):
        to = (lax.rem(pair + j, pairs) * 2 + core, r)
        return remote(
            x_hbm.at[0, pl.ds(c * chunk, chunk)], xs.at[rows_of(t, c)],
            cross_send.at[j, c], cross_recv.at[j, c], to,
        )

    def crossed(j, c):
        return xs.at[rows_of(lax.rem(pair - j + pairs, pairs) * 2 + core, c)]

    def arrived(j, c):
        place = crossed(j, c)
        return remote(place, place, cross_send.at[j, c], cross_recv.at[j, c], mate)

    def own_to_mate(c):
        return remote(
            x_hbm.at[0, pl.ds(c * chunk, chunk)], xs.at[rows_of(t, c)],
            core_send.at[0, c], core_recv.at[0, c], mate,
        )

    def relay(j, c):
        place = crossed(j, c)
        return remote(place, place, core_send.at[j, c], core_recv.at[j, c], mate)

    def from_mate(j, c):
        source = lax.rem(pair - j + pairs, pairs) * 2 + 1 - core
        place = xs.at[rows_of(source, c)]
        return remote(place, place, core_send.at[j, c], core_recv.at[j, c], mate)

    def w_scatter(j):
        to = lax.rem(t + j, tasks)
        return remote(wt_send.at[to], wt_all.at[t], w_send_sem.at[j], w_recv_sem.at[j], (to, r))

    def y_scatter(k):
        to = lax.rem(r + k, rows)
        return remote(y_send.at[to], y_recv.at[k], yr_send.at[k], yr_recv.at[k], (t, to))

    for j in range(1, pairs):
        cross(j, 0).start()
    for k in range(1, rows):
        y_scatter(k).start()
    for c in range(1, CHUNKS):
        for j in range(1, pairs):
            cross(j, c).start()
        if c == 1:
            for j in range(1, tasks):
                w_scatter(j).start()
    for c in range(CHUNKS):
        own_to_mate(c).start()

    total_y = y_send[r]
    for k in range(1, rows):
        y_scatter(k).wait_recv()
        total_y = total_y + y_recv[k]
    y_red[...] = total_y
    owner = r // per
    place_y = y_all.at[
        pl.ds(pl.multiple_of(lax.rem(r, per) * piece, piece), piece),
        pl.ds(pl.multiple_of(t * probe, LANES), probe),
    ]

    def y_gather(k):
        return remote(
            y_red, place_y, ya_send.at[k], ya_recv.at[t * per + lax.rem(r, per)],
            (owner, lax.rem(r + k, rows)),
        )

    for k in range(1, rows):
        y_gather(k).start()

    @pl.when(owner != t)
    def _():
        y_gather(0).start()

    @pl.when(owner == t)
    def _():
        y_all[
            pl.ds(pl.multiple_of(lax.rem(r, per) * piece, piece), piece),
            pl.ds(pl.multiple_of(t * probe, LANES), probe),
        ] = total_y

    def pass_on(j, c):
        arrived(j, c).wait_recv()
        relay(j, c).start()
        source = lax.rem(pair - j + pairs, pairs) * 2 + core
        part = row_squares(source * probe + c * chunk, chunk)
        squares[source] = part if c == 0 else squares[source] + part

    def take_in(j, c):
        from_mate(j, c).wait_recv()
        source = lax.rem(pair - j + pairs, pairs) * 2 + 1 - core
        part = row_squares(source * probe + c * chunk, chunk)
        squares[source] = part if c == 0 else squares[source] + part

    for c in range(CHUNKS):
        take_in(0, c)
    for c in range(CHUNKS // 2):
        for j in range(1, pairs):
            pass_on(j, c)
    for task in range(tasks):
        for k in range(per):

            @pl.when(jnp.logical_or(task != t, t * per + k != r))
            def _():
                place = y_all.at[pl.ds(k * piece, piece), pl.ds(task * probe, probe)]
                remote(
                    y_red, place, ya_send.at[0], ya_recv.at[task * per + k], (t, r)
                ).wait_recv()

    for j in range(1, tasks):
        source = lax.rem(t - j + tasks, tasks)
        remote(
            wt_send.at[0], wt_all.at[source], w_send_sem.at[j], w_recv_sem.at[j], (t, r)
        ).wait_recv()
    for c in range(CHUNKS // 2, CHUNKS):
        for j in range(1, pairs):
            pass_on(j, c)
            take_in(j, c - CHUNKS // 2)
    for c in range(CHUNKS - CHUNKS // 2, CHUNKS):
        for j in range(1, pairs):
            take_in(j, c)

    diag = jnp.zeros((1, width), F32)
    term = jnp.zeros((group, width), F32)
    for task in range(tasks):
        own_diag = jnp.sum(squares[task], axis=0, keepdims=True)
        diag = diag + own_diag
        term = term + own_diag * wt_all[task].astype(F32)
    diag = c2 * diag
    targets = c1 * times_probes(y_all[...], xs) + c2 * term

    lane = lax.broadcasted_iota(jnp.int32, (group, LANES), 1)

    def reduce_rows(n, vector, sums):
        extra = jnp.zeros((group, LANES), F32)
        for i, value in enumerate(sums):
            extra = jnp.where(lane == i, value, extra)
        extra = jnp.concatenate([extra, jnp.zeros((LANES - group, LANES), F32)], axis=0).T[:SUB]
        terms = two_terms(vector)

        def scatter(to):
            k = lax.rem(to - r + rows, rows)
            return remote(
                z_send.at[n, to], z_recv.at[n, k], zr_send.at[n, k], zr_recv.at[n, k], (t, to)
            )

        for p in range(parts):
            product = fold(
                lax.dot_general(
                    terms, xs[p * span : (p + 1) * span, :], (((1,), (1,)), ((), ())),
                    preferred_element_type=F32,
                )
            )
            for q in range(p, rows, parts):
                top = SUB * (q // parts)
                z_send[n, q, :, :span] = product[top : top + SUB]
                z_send[n, q, :, span:] = extra

                @pl.when(q != r)
                def _():
                    scatter(q).start()

        acc = z_send[n, r]
        for k in range(1, rows):
            remote(
                z_send.at[n, r], z_recv.at[n, k], zr_send.at[n, k], zr_recv.at[n, k], (t, r)
            ).wait_recv()
            acc = acc + z_recv[n, k]
        z_red[n] = acc[:, :span]

        def spot(source):
            return (
                n,
                pl.ds(pl.multiple_of(SUB * (source // parts), SUB), SUB),
                pl.ds(pl.multiple_of(span * lax.rem(source, parts), LANES), span),
            )

        def gather(k):
            return remote(
                z_red.at[n], z_flat.at[spot(r)], za_send.at[n, k], za_recv.at[n, k],
                (t, lax.rem(r + k, rows)),
            )

        for k in range(1, rows):
            gather(k).start()
        z_flat[spot(r)] = acc[:, :span]
        found = jnp.concatenate([acc[:, span:], jnp.zeros((LANES - SUB, LANES), F32)], axis=0).T
        for k in range(1, rows):
            source = lax.rem(r - k + rows, rows)
            remote(
                z_red.at[n], z_flat.at[spot(source)], za_send.at[n, k], za_recv.at[n, k], (t, r)
            ).wait_recv()
        for k in range(1, rows):
            scatter(lax.rem(r + k, rows)).wait_send()
            gather(k).wait_send()
        return z_flat[n], [found[:group, i : i + 1] for i in range(len(sums))]

    def column_sum(value):
        return jnp.sum(value, axis=1, keepdims=True)

    product, (norm_0, weighted_00) = reduce_rows(
        0,
        targets,
        [column_sum(targets * targets), column_sum(diag * targets * targets)],
    )
    step_1 = norm_0 / (c1 * column_sum(product * product) + weighted_00)
    residual = targets - step_1 * (c1 * times_probes(product, xs) + diag * targets)

    weighted = diag * residual
    product_r, (norm_1, weighted_11, weighted_01) = reduce_rows(
        1,
        residual,
        [column_sum(residual * residual), column_sum(weighted * residual), column_sum(weighted * targets)],
    )
    beta = norm_1 / (norm_0 + EPS)
    product = product_r + beta * product
    direction = residual + beta * targets
    curve = c1 * column_sum(product * product) + (
        weighted_11 + beta * (2.0 * weighted_01 + beta * weighted_00)
    )
    step_2 = norm_1 / curve

    def finish(n, value):
        for q in range(tasks):
            fin_send[n, q, :, :share] = value[:, q * share : (q + 1) * share]
        for j in range(1, tasks):
            to = lax.rem(t + j, tasks)
            remote(
                fin_send.at[n, to], fin_recv.at[n, t], f_send.at[n, j], f_recv.at[n, j], (to, r)
            ).start()
        fin_recv[n, t] = fin_send[n, t]

    def collect(n, out_ref):
        for j in range(1, tasks):
            source = lax.rem(t - j + tasks, tasks)
            remote(
                fin_send.at[n, source], fin_recv.at[n, source], f_send.at[n, j], f_recv.at[n, j], (t, r)
            ).wait()
        whole = fin_recv[n].reshape(cols, fin_recv.shape[3]).T
        out_ref[...] = whole[:share]

    finish(0, step_1 * targets + step_2 * direction)
    finish(1, residual - step_2 * (c1 * times_probes(product, xs) + diag * direction))
    for c in range(CHUNKS):
        own_to_mate(c).wait_send()
        for j in range(1, pairs):
            cross(j, c).wait_send()
            relay(j, c).wait_send()
    for k in range(1, rows):
        y_scatter(k).wait_send()
        y_gather(k).wait_send()

    @pl.when(owner != t)
    def _():
        y_gather(0).wait_send()

    for j in range(1, tasks):
        w_scatter(j).wait_send()
    collect(0, merged_ref)
    collect(1, residual_ref)


def on_device(tasks, rows, probes, task_weights):
    probe, width = probes.shape[1:]
    cols = task_weights.shape[2]
    group = cols // tasks
    piece = cols // rows
    per = group // piece
    parts = rows // (group // SUB)
    span = tasks * probe // parts
    share = width // tasks
    pairs = tasks // 2
    padded = max(share, LANES)
    w_type = BF16 if group % 16 == 0 else F32
    vmem, dma = pltpu.VMEM, pltpu.SemaphoreType.DMA
    merged, residual = pl.pallas_call(
        functools.partial(kernel, tasks, rows),
        out_shape=[jax.ShapeDtypeStruct((share, cols), F32)] * 2,
        in_specs=[pl.BlockSpec(memory_space=pltpu.HBM)] * 2,
        out_specs=[pl.BlockSpec(memory_space=pltpu.VMEM)] * 2,
        scratch_shapes=[
            vmem((tasks * probe, width), BF16),
            vmem((width, cols), BF16),
            vmem((tasks, group, width), w_type),
            vmem((tasks, group, width), w_type),
            vmem((rows, piece, probe), F32),
            vmem((rows, piece, probe), F32),
            vmem((piece, probe), F32),
            vmem((group, tasks * probe), F32),
            vmem((tasks, 16, width), F32),
            vmem((2, rows, SUB, span + LANES), F32),
            vmem((2, rows, SUB, span + LANES), F32),
            vmem((2, SUB, span), F32),
            vmem((2, group, tasks * probe), F32),
            vmem((2, tasks, group, padded), F32),
            vmem((2, tasks, group, padded), F32),
            dma((2,)),
            dma((pairs, CHUNKS)),
            dma((pairs, CHUNKS)),
            dma((pairs, CHUNKS)),
            dma((pairs, CHUNKS)),
            dma((tasks,)),
            dma((tasks,)),
            dma((rows,)),
            dma((rows,)),
            dma((rows,)),
            dma((tasks * per,)),
            dma((2, rows)),
            dma((2, rows)),
            dma((2, rows)),
            dma((2, rows)),
            dma((2, tasks)),
            dma((2, tasks)),
        ],
        compiler_params=pltpu.CompilerParams(
            collective_id=0, has_side_effects=True, vmem_limit_bytes=48 * 2**20
        ),
    )(probes, task_weights)
    return merged, residual


def solution(mesh):
    in_specs = (P("task", None, "rows"), P("task", "rows", None))
    out_specs = (P(("rows", "task"), None), P(("rows", "task"), None))
    body = functools.partial(on_device, mesh.shape["task"], mesh.shape["rows"])
    return jax.shard_map(body, mesh=mesh, in_specs=in_specs, out_specs=out_specs, check_vma=False)
```

```python
import functools

import jax
import jax.numpy as jnp
from jax import lax
from jax.experimental import pallas as pl
from jax.experimental.pallas import tpu as pltpu
from jax.sharding import PartitionSpec as P

ALPHA = 0.9
EPS = 1e-06
LANES = 128
SUB = 8
CHUNKS = 6
F32 = jnp.float32
BF16 = jnp.bfloat16
MESH = pl.DeviceIdType.MESH


def two_terms(value):
    high = value.astype(BF16).astype(F32)
    return jnp.concatenate([high, value - high], axis=0).astype(BF16)


def fold(product):
    half = product.shape[0] // 2
    return product[:half] + product[half:]


def times_probes(value, xs):
    return fold(jnp.dot(two_terms(value), xs[...], preferred_element_type=F32))


def remote(src, dst, send, recv, device):
    return pltpu.make_async_remote_copy(
        src_ref=src, dst_ref=dst, send_sem=send, recv_sem=recv, device_id=device, device_id_type=MESH
    )


def kernel(
    tasks, rows,
    x_hbm, w_hbm, merged_ref, residual_ref,
    xs, w_own, wt_send, wt_all, y_send, y_recv, y_red, y_all,
    squares, z_send, z_recv, z_red, z_flat, fin_send, fin_recv,
    local_sem, cross_send, cross_recv, core_send, core_recv, w_send_sem, w_recv_sem,
    yr_send, yr_recv, ya_send, ya_recv, zr_send, zr_recv, za_send, za_recv, f_send, f_recv,
):
    t, r = lax.axis_index("task"), lax.axis_index("rows")
    probe, width = x_hbm.shape[1:]
    cols = w_hbm.shape[2]
    group = cols // tasks
    piece = cols // rows
    per = group // piece
    parts = rows // (group // SUB)
    span = tasks * probe // parts
    share = width // tasks
    pairs = tasks // 2
    chunk = probe // CHUNKS
    c1 = ALPHA / (probe * tasks)
    c2 = (1.0 - ALPHA) / (probe * tasks)

    barrier = pltpu.get_barrier_semaphore()

    @pl.loop(1, tasks)
    def _(i):
        pl.semaphore_signal(
            barrier, inc=1, device_id=(lax.rem(t + i, tasks), r), device_id_type=MESH
        )

    @pl.loop(1, rows)
    def _(i):
        pl.semaphore_signal(
            barrier, inc=1, device_id=(t, lax.rem(r + i, rows)), device_id_type=MESH
        )

    load_x = pltpu.make_async_copy(
        x_hbm.at[0], xs.at[pl.ds(pl.multiple_of(t * probe, probe), probe)], local_sem.at[0]
    )
    load_x.start()
    load_w = pltpu.make_async_copy(w_hbm.at[0], w_own, local_sem.at[1])
    load_w.start()

    def row_squares(first, count):
        def add(i, acc):
            block = xs[pl.ds(pl.multiple_of(first + i * 16, 16), 16), :].astype(F32)
            return acc + block * block

        return lax.fori_loop(0, count // 16, add, jnp.zeros((16, width), F32))

    load_w.wait()
    wt_send[...] = w_own[...].astype(F32).T.reshape(wt_send.shape).astype(wt_send.dtype)
    wt_all[t] = wt_send[t]
    load_x.wait()
    own = xs[pl.ds(pl.multiple_of(t * probe, probe), probe), :]
    outputs = jnp.dot(own, w_own[...], preferred_element_type=F32)
    y_send[...] = outputs.T.reshape(y_send.shape)
    squares[t] = row_squares(t * probe, probe)
    pl.semaphore_wait(barrier, tasks + rows - 2)

    pair, core = t // 2, lax.rem(t, 2)
    mate = (pair * 2 + 1 - core, r)

    def rows_of(task, c):
        return pl.ds(pl.multiple_of(task * probe + c * chunk, chunk), chunk)

    def cross(j, c):
        to = (lax.rem(pair + j, pairs) * 2 + core, r)
        return remote(
            xs.at[rows_of(t, c)], xs.at[rows_of(t, c)],
            cross_send.at[j, c], cross_recv.at[j, c], to,
        )

    def crossed(j, c):
        return xs.at[rows_of(lax.rem(pair - j + pairs, pairs) * 2 + core, c)]

    def arrived(j, c):
        place = crossed(j, c)
        return remote(place, place, cross_send.at[j, c], cross_recv.at[j, c], mate)

    def own_to_mate(c):
        return remote(
            xs.at[rows_of(t, c)], xs.at[rows_of(t, c)],
            core_send.at[0, c], core_recv.at[0, c], mate,
        )

    def relay(j, c):
        place = crossed(j, c)
        return remote(place, place, core_send.at[j, c], core_recv.at[j, c], mate)

    def from_mate(j, c):
        source = lax.rem(pair - j + pairs, pairs) * 2 + 1 - core
        place = xs.at[rows_of(source, c)]
        return remote(place, place, core_send.at[j, c], core_recv.at[j, c], mate)

    def w_scatter(j):
        to = lax.rem(t + j, tasks)
        return remote(wt_send.at[to], wt_all.at[t], w_send_sem.at[j], w_recv_sem.at[j], (to, r))

    def y_scatter(k):
        to = lax.rem(r + k, rows)
        return remote(y_send.at[to], y_recv.at[k], yr_send.at[k], yr_recv.at[k], (t, to))

    for j in range(1, pairs):
        cross(j, 0).start()
    for k in range(1, rows):
        y_scatter(k).start()
    for c in range(1, CHUNKS):
        for j in range(1, pairs):
            cross(j, c).start()
        if c == 1:
            for j in range(1, tasks):
                w_scatter(j).start()
    for c in range(CHUNKS):
        own_to_mate(c).start()

    total_y = y_send[r]
    for k in range(1, rows):
        y_scatter(k).wait_recv()
        total_y = total_y + y_recv[k]
    y_red[...] = total_y
    owner = r // per
    place_y = y_all.at[
        pl.ds(pl.multiple_of(lax.rem(r, per) * piece, piece), piece),
        pl.ds(pl.multiple_of(t * probe, LANES), probe),
    ]

    def y_gather(k):
        return remote(
            y_red, place_y, ya_send.at[k], ya_recv.at[t * per + lax.rem(r, per)],
            (owner, lax.rem(r + k, rows)),
        )

    for k in range(1, rows):
        y_gather(k).start()

    @pl.when(owner != t)
    def _():
        y_gather(0).start()

    @pl.when(owner == t)
    def _():
        y_all[
            pl.ds(pl.multiple_of(lax.rem(r, per) * piece, piece), piece),
            pl.ds(pl.multiple_of(t * probe, LANES), probe),
        ] = total_y

    def pass_on(j, c):
        arrived(j, c).wait_recv()
        relay(j, c).start()
        source = lax.rem(pair - j + pairs, pairs) * 2 + core
        part = row_squares(source * probe + c * chunk, chunk)
        squares[source] = part if c == 0 else squares[source] + part

    def take_in(j, c):
        from_mate(j, c).wait_recv()
        source = lax.rem(pair - j + pairs, pairs) * 2 + 1 - core
        part = row_squares(source * probe + c * chunk, chunk)
        squares[source] = part if c == 0 else squares[source] + part

    for c in range(CHUNKS):
        take_in(0, c)
    for c in range(CHUNKS // 2):
        for j in range(1, pairs):
            pass_on(j, c)
    for task in range(tasks):
        for k in range(per):

            @pl.when(jnp.logical_or(task != t, t * per + k != r))
            def _():
                place = y_all.at[pl.ds(k * piece, piece), pl.ds(task * probe, probe)]
                remote(
                    y_red, place, ya_send.at[0], ya_recv.at[task * per + k], (t, r)
                ).wait_recv()

    for j in range(1, tasks):
        source = lax.rem(t - j + tasks, tasks)
        remote(
            wt_send.at[0], wt_all.at[source], w_send_sem.at[j], w_recv_sem.at[j], (t, r)
        ).wait_recv()
    for c in range(CHUNKS // 2, CHUNKS):
        for j in range(1, pairs):
            pass_on(j, c)
            take_in(j, c - CHUNKS // 2)
    for c in range(CHUNKS - CHUNKS // 2, CHUNKS):
        for j in range(1, pairs):
            take_in(j, c)

    diag = jnp.zeros((1, width), F32)
    term = jnp.zeros((group, width), F32)
    for task in range(tasks):
        own_diag = jnp.sum(squares[task], axis=0, keepdims=True)
        diag = diag + own_diag
        term = term + own_diag * wt_all[task].astype(F32)
    diag = c2 * diag
    targets = c1 * times_probes(y_all[...], xs) + c2 * term

    lane = lax.broadcasted_iota(jnp.int32, (group, LANES), 1)

    def reduce_rows(n, vector, sums):
        extra = jnp.zeros((group, LANES), F32)
        for i, value in enumerate(sums):
            extra = jnp.where(lane == i, value, extra)
        extra = jnp.concatenate([extra, jnp.zeros((LANES - group, LANES), F32)], axis=0).T[:SUB]
        terms = two_terms(vector)

        def scatter(to):
            k = lax.rem(to - r + rows, rows)
            return remote(
                z_send.at[n, to], z_recv.at[n, k], zr_send.at[n, k], zr_recv.at[n, k], (t, to)
            )

        for p in range(parts):
            product = fold(
                lax.dot_general(
                    terms, xs[p * span : (p + 1) * span, :], (((1,), (1,)), ((), ())),
                    preferred_element_type=F32,
                )
            )
            for q in range(p, rows, parts):
                top = SUB * (q // parts)
                z_send[n, q, :, :span] = product[top : top + SUB]
                z_send[n, q, :, span:] = extra

                @pl.when(q != r)
                def _():
                    scatter(q).start()

        acc = z_send[n, r]
        for k in range(1, rows):
            remote(
                z_send.at[n, r], z_recv.at[n, k], zr_send.at[n, k], zr_recv.at[n, k], (t, r)
            ).wait_recv()
            acc = acc + z_recv[n, k]
        z_red[n] = acc[:, :span]

        def spot(source):
            return (
                n,
                pl.ds(pl.multiple_of(SUB * (source // parts), SUB), SUB),
                pl.ds(pl.multiple_of(span * lax.rem(source, parts), LANES), span),
            )

        def gather(k):
            return remote(
                z_red.at[n], z_flat.at[spot(r)], za_send.at[n, k], za_recv.at[n, k],
                (t, lax.rem(r + k, rows)),
            )

        for k in range(1, rows):
            gather(k).start()
        z_flat[spot(r)] = acc[:, :span]
        found = jnp.concatenate([acc[:, span:], jnp.zeros((LANES - SUB, LANES), F32)], axis=0).T
        for k in range(1, rows):
            source = lax.rem(r - k + rows, rows)
            remote(
                z_red.at[n], z_flat.at[spot(source)], za_send.at[n, k], za_recv.at[n, k], (t, r)
            ).wait_recv()
        for k in range(1, rows):
            scatter(lax.rem(r + k, rows)).wait_send()
            gather(k).wait_send()
        return z_flat[n], [found[:group, i : i + 1] for i in range(len(sums))]

    def column_sum(value):
        return jnp.sum(value, axis=1, keepdims=True)

    product, (norm_0, weighted_00) = reduce_rows(
        0,
        targets,
        [column_sum(targets * targets), column_sum(diag * targets * targets)],
    )
    step_1 = norm_0 / (c1 * column_sum(product * product) + weighted_00)
    residual = targets - step_1 * (c1 * times_probes(product, xs) + diag * targets)

    weighted = diag * residual
    product_r, (norm_1, weighted_11, weighted_01) = reduce_rows(
        1,
        residual,
        [column_sum(residual * residual), column_sum(weighted * residual), column_sum(weighted * targets)],
    )
    beta = norm_1 / (norm_0 + EPS)
    product = product_r + beta * product
    direction = residual + beta * targets
    curve = c1 * column_sum(product * product) + (
        weighted_11 + beta * (2.0 * weighted_01 + beta * weighted_00)
    )
    step_2 = norm_1 / curve

    def finish(n, value):
        for q in range(tasks):
            fin_send[n, q, :, :share] = value[:, q * share : (q + 1) * share]
        for j in range(1, tasks):
            to = lax.rem(t + j, tasks)
            remote(
                fin_send.at[n, to], fin_recv.at[n, t], f_send.at[n, j], f_recv.at[n, j], (to, r)
            ).start()
        fin_recv[n, t] = fin_send[n, t]

    def collect(n, out_ref):
        for j in range(1, tasks):
            source = lax.rem(t - j + tasks, tasks)
            remote(
                fin_send.at[n, source], fin_recv.at[n, source], f_send.at[n, j], f_recv.at[n, j], (t, r)
            ).wait()
        whole = fin_recv[n].reshape(cols, fin_recv.shape[3]).T
        out_ref[...] = whole[:share]

    finish(0, step_1 * targets + step_2 * direction)
    finish(1, residual - step_2 * (c1 * times_probes(product, xs) + diag * direction))
    for c in range(CHUNKS):
        own_to_mate(c).wait_send()
        for j in range(1, pairs):
            cross(j, c).wait_send()
            relay(j, c).wait_send()
    for k in range(1, rows):
        y_scatter(k).wait_send()
        y_gather(k).wait_send()

    @pl.when(owner != t)
    def _():
        y_gather(0).wait_send()

    for j in range(1, tasks):
        w_scatter(j).wait_send()
    collect(0, merged_ref)
    collect(1, residual_ref)


def on_device(tasks, rows, probes, task_weights):
    probe, width = probes.shape[1:]
    cols = task_weights.shape[2]
    group = cols // tasks
    piece = cols // rows
    per = group // piece
    parts = rows // (group // SUB)
    span = tasks * probe // parts
    share = width // tasks
    pairs = tasks // 2
    padded = max(share, LANES)
    w_type = BF16 if group % 16 == 0 else F32
    vmem, dma = pltpu.VMEM, pltpu.SemaphoreType.DMA
    merged, residual = pl.pallas_call(
        functools.partial(kernel, tasks, rows),
        out_shape=[jax.ShapeDtypeStruct((share, cols), F32)] * 2,
        in_specs=[pl.BlockSpec(memory_space=pltpu.HBM)] * 2,
        out_specs=[pl.BlockSpec(memory_space=pltpu.VMEM)] * 2,
        scratch_shapes=[
            vmem((tasks * probe, width), BF16),
            vmem((width, cols), BF16),
            vmem((tasks, group, width), w_type),
            vmem((tasks, group, width), w_type),
            vmem((rows, piece, probe), F32),
            vmem((rows, piece, probe), F32),
            vmem((piece, probe), F32),
            vmem((group, tasks * probe), F32),
            vmem((tasks, 16, width), F32),
            vmem((2, rows, SUB, span + LANES), F32),
            vmem((2, rows, SUB, span + LANES), F32),
            vmem((2, SUB, span), F32),
            vmem((2, group, tasks * probe), F32),
            vmem((2, tasks, group, padded), F32),
            vmem((2, tasks, group, padded), F32),
            dma((2,)),
            dma((pairs, CHUNKS)),
            dma((pairs, CHUNKS)),
            dma((pairs, CHUNKS)),
            dma((pairs, CHUNKS)),
            dma((tasks,)),
            dma((tasks,)),
            dma((rows,)),
            dma((rows,)),
            dma((rows,)),
            dma((tasks * per,)),
            dma((2, rows)),
            dma((2, rows)),
            dma((2, rows)),
            dma((2, rows)),
            dma((2, tasks)),
            dma((2, tasks)),
        ],
        compiler_params=pltpu.CompilerParams(
            collective_id=0, has_side_effects=True, vmem_limit_bytes=62 * 2**20
        ),
    )(probes, task_weights)
    return merged, residual


def solution(mesh):
    in_specs = (P("task", None, "rows"), P("task", "rows", None))
    out_specs = (P(("rows", "task"), None), P(("rows", "task"), None))
    body = functools.partial(on_device, mesh.shape["task"], mesh.shape["rows"])
    return jax.shard_map(body, mesh=mesh, in_specs=in_specs, out_specs=out_specs, check_vma=False)
```
